128 devices in a mesh: kr: 8 (over z, core), kc: 16 (over y, x).
Axes of the slice: x: 4, y: 4, z: 4, core: 2. Of those that a mesh axis runs over, the one named last changes fastest.
Arguments:
- trial: bfloat16 [256, 512], P(('kr', 'kc')), may hold values from -6 to 6
- screened: bfloat16 [16, 2048, 2048], P(None, None, 'kc'), may hold values from -0.125 to 0.125
- density: bfloat16 [4096, 2048, 128], P(('kr', 'kc')), may hold values from -0.15625 to 0.15625
- pair_rows: int32 [4096], P(('kr', 'kc')), may hold values from 0 to 31
- pair_cols: int32 [4096], P(('kr', 'kc')), may hold values from 0 to 15
- slot_momentum: int32 [256], P(('kr', 'kc')), may hold values from 0 to 15
- slot_count: int32 [256], P(('kr', 'kc')), may hold values from 1 to 16, as said below
Outputs:
- response: float32 [256, 512], P(('kr', 'kc'))
The draws below stay inside these ranges and needn't reach their ends.
Inputs may be any that keep to these rules, and one draw needn't show every extreme that they name: `slot_count`: the first transfer slot always holds 16 listed pairs.
All inputs are finite; a program needn't handle non-finite values.
Results may differ from the reference program's by a relative error of at most 0.0029.
Values may be sent and summed in bfloat16 or wider, within the bound.
A program may use at most 192 MiB of HBM per device.

```python
import jax
import jax.numpy as jnp
from jax import lax

G = 2048
NCON = 8
NVAL = 8
NV = 8
MOMENTUM_COUNT = 16
QSLOT = 2
PAIRS_PER_SLOT = 16
KB = 2
NK = 256
KROW = 32
KCOL = 16
PAIRS_DEV = 32
NPAIR = 4096
TRANSFER_SLOTS = 256
CVN = 512
DENS = 128
N_KR = 8
N_KC = 16


def draw_slot_count(key, part):
    key = jax.random.fold_in(key, 7)
    tally_count = jax.random.randint(key, (TRANSFER_SLOTS,), 1, PAIRS_PER_SLOT + 1)
    return jnp.where(jnp.arange(TRANSFER_SLOTS) == 0, PAIRS_PER_SLOT, tally_count).astype(jnp.int32)


def touch_ends(entries, key, least, high):
    index_at = [jax.random.randint(jax.random.fold_in(key, axis), (), 0, length) for axis, length in enumerate(entries.shape)]
    longest = entries.shape.index(max(entries.shape))
    beside = index_at[:longest] + [(index_at[longest] + 1) % entries.shape[longest]] + index_at[longest + 1:]
    return entries.at[tuple(index_at)].set(least).at[tuple(beside)].set(high)


def levels(stream_key, extent, pieces, least, largest):
    gain = 1.0
    for position, shards_of in pieces:
        draws = jax.random.uniform(jax.random.fold_in(jax.random.fold_in(stream_key, 6), position), (shards_of,), jnp.float32, least / len(pieces), largest / len(pieces))
        gain = gain * jnp.repeat(jnp.exp(draws), extent[position] // shards_of).reshape((-1,) + (1,) * (len(extent) - 1 - position))
    return gain


def normal_values(own_key, dims, spread, limit, split=(), kind=jnp.bfloat16):
    entries = jax.random.normal(own_key, dims, jnp.float32) * spread
    if len(split) > 0:
        entries = levels(own_key, dims, split, -0.22, 0.18) * entries
    return jnp.clip(entries, min=-limit, max=limit).astype(kind)


def setup_inputs(seed: int = 0) -> dict:
    keys = jax.random.split(jax.random.key(seed), 8)
    return {
        "trial": normal_values(keys[0], (NK, CVN), 1.0, 6.0, ((0, 128),)),
        "screened": normal_values(keys[1], (MOMENTUM_COUNT, G, G), G ** -0.5, 0.125, ((2, 16),)),
        "density": normal_values(keys[2], (NPAIR, G, DENS), (1.0 / (32.0 * G ** 0.5) ** 0.5), 0.15625, ((0, 128),)),
        "pair_rows": touch_ends(jax.random.randint(keys[3], (NPAIR,), 0, KROW), jax.random.fold_in(keys[3], 1), 0, KROW - 1).astype(jnp.int32),
        "pair_cols": touch_ends(jax.random.randint(keys[4], (NPAIR,), 0, KCOL), jax.random.fold_in(keys[4], 1), 0, KCOL - 1).astype(jnp.int32),
        "slot_momentum": touch_ends(jax.random.randint(keys[5], (TRANSFER_SLOTS,), 0, MOMENTUM_COUNT), jax.random.fold_in(keys[5], 1), 0, MOMENTUM_COUNT - 1).astype(jnp.int32),
        "slot_count": draw_slot_count(jax.random.fold_in(keys[7], 71), 0),
    }


def reference(trial, screened, density, pair_rows, pair_cols, slot_momentum, slot_count):
    cond_width = NCON * NCON
    high = lax.Precision.HIGHEST

    def one_device(accumulated, device):
        band_row = device // N_KC
        band_col = device % N_KC
        densities = lax.dynamic_slice_in_dim(density, device * PAIRS_DEV, PAIRS_DEV, 0).astype(jnp.float32)
        densities = densities.reshape(QSLOT, PAIRS_PER_SLOT, G, DENS)
        slot_ids = lax.dynamic_slice_in_dim(slot_momentum, device * QSLOT, QSLOT, 0)
        tally_count = lax.dynamic_slice_in_dim(slot_count, device * QSLOT, QSLOT, 0)
        weights = jnp.take(screened, slot_ids, axis=0).astype(jnp.float32)
        conduction = densities[..., :cond_width]
        valence = densities[..., cond_width:]
        screened_val = jnp.einsum('sgh,sphw->spwg', weights, valence, precision=high).astype(jnp.bfloat16)
        screened_val = lax.optimization_barrier(screened_val).astype(jnp.float32)
        direct_kernel = jnp.einsum('spgi,spwg->spiw', conduction, screened_val, precision=high)
        live_mask = jnp.arange(PAIRS_PER_SLOT, dtype=jnp.int32)[None, :] < tally_count[:, None]
        direct_kernel = jnp.where(live_mask[:, :, None, None], direct_kernel, jnp.float32(0.0))
        direct_kernel = direct_kernel.reshape(PAIRS_DEV, NCON, NCON, NVAL, NVAL)
        row_local = lax.dynamic_slice_in_dim(pair_rows, device * PAIRS_DEV, PAIRS_DEV, 0)
        col_local = lax.dynamic_slice_in_dim(pair_cols, device * PAIRS_DEV, PAIRS_DEV, 0)
        k_glob = (band_row * KROW + row_local).astype(jnp.int32)
        kp_glob = (((col_local // KB) * N_KC + band_col) * KB + col_local % KB).astype(jnp.int32)
        trial_row = jnp.take(trial, k_glob, axis=0).astype(jnp.float32).reshape(PAIRS_DEV, NCON, NVAL, NV)
        vec_col = jnp.take(trial, kp_glob, axis=0).astype(jnp.float32).reshape(PAIRS_DEV, NCON, NVAL, NV)
        y_row = jnp.einsum('pcdvw,pdwn->pcvn', direct_kernel, vec_col, precision=high).reshape(PAIRS_DEV, CVN)
        y_col = jnp.einsum('pcdvw,pcvn->pdwn', direct_kernel, trial_row, precision=high).reshape(PAIRS_DEV, CVN)
        accumulated = accumulated.at[k_glob].add(y_row)
        accumulated = accumulated.at[kp_glob].add(y_col)
        return accumulated, None

    start = jnp.zeros((NK, CVN), jnp.float32)
    result, unused = lax.scan(one_device, start, jnp.arange(N_KR * N_KC, dtype=jnp.int32))
    return result
```

```python
import functools

import jax
import jax.numpy as jnp
from jax import lax
from jax.experimental import pallas as pl
from jax.experimental.pallas import tpu as pltpu
from jax.sharding import PartitionSpec as P

MESH = pl.DeviceIdType.MESH
F32 = jnp.float32
BF = jnp.bfloat16
NU = 8
NC = 4
RC = 64
PLANE_ROWS = 1024

SEQ = (
    "S00", "S01", "S10", "T00", "P0", "S20", "S11", "P1", "S02", "S30",
    "M0", "P2", "S21", "S12", "S03", "P3", "S40", "S31", "S22", "S13",
    "T01", "P4", "S41", "S32", "S23", "T10", "P5", "S42", "S33", "T20",
    "T11", "T02", "P6", "S43", "P7", "T21", "T12", "T03", "X0", "Y0",
    "C0", "T22", "C1", "T13", "E0", "T23", "C2", "E1", "C3", "E2",
    "E3",
)


def kernel(w, dens, mom, count, rows, cols, trial, out, momv, moml, moms, *scratch):
    ag_b, ag_1, ag_2 = scratch[:NU], scratch[NU:NU + NC], scratch[NU + NC:NU + 2 * NC]
    (
        st_b, land_b, land_1, land_2,
        rv, rcd, kacc, xr, xc, xf, br, bc, pick_r, pick_c, kd, sum_r, sum_c, land_r, land_c,
        msend, mrecv, bsend, brecv, dsend, drecv, asend, arecv, xsend, xrecv, ysend, yrecv, lsem, psem,
    ) = scratch[NU + 2 * NC:]
    kr = lax.axis_index("kr")
    kc = lax.axis_index("kc")
    z, c, y, x = kr // 2, kr % 2, kc // 4, kc % 4

    def dev(x_, y_, z_, c_):
        return (z_ * 2 + c_, y_ * 4 + x_)

    def member(g, d):
        a, cc = d // 2, d % 2
        return (dev(x, y, a, cc), dev(a, y, z, cc), dev(x, a, z, cc))[g]

    mine = (z * 2 + c, x * 2 + c, y * 2 + c)
    xp, xm, yp, ym = (x + 1) % 4, (x + 3) % 4, (y + 1) % 4, (y + 3) % 4
    to_x = (dev(xp, y, z, c), dev(xm, y, z, c))
    to_y = (dev(x, yp, z, c), dev(x, ym, z, c))

    def copy_to(src, dst, ss, rs, to):
        return pltpu.make_async_remote_copy(
            src_ref=src, dst_ref=dst, send_sem=ss, recv_sem=rs, device_id=to, device_id_type=MESH
        )

    sent = []
    left = set()

    def go(copies):
        for cp in copies:
            cp.start()
            sent.append(cp)
        return copies

    def local(src, dst, sem):
        cp = pltpu.make_async_copy(src, dst, sem)
        cp.start()
        return cp

    def rows_b(u):
        return pl.ds(pl.multiple_of(kr * (NU * 16) + u * 16, 16), 16)

    def rows_d(p, h):
        return pl.ds(pl.multiple_of(PLANE_ROWS + p * 512 + c * 256 + h * RC, 16), RC)

    own_b = [local(w.at[:, rows_b(u)], ag_b[u].at[y, x], lsem.at[u]) for u in range(NU)]
    own_d = [
        [local(w.at[:, rows_d(0, h)], ag_1[h].at[y], lsem.at[NU + h]) for h in range(NC)],
        [local(w.at[:, rows_d(1, h)], ag_2[h].at[x], lsem.at[NU + NC + h]) for h in range(NC)],
    ]
    dens_in = []
    for b in range(8):
        for half in range(2):
            pair = (b * 2 + half) * 2
            lanes = pl.ds(half * 128, 128)
            dens_in.append((
                local(dens.at[pair], rcd.at[b, :, :, lanes], psem.at[pair]),
                local(dens.at[pair + 1], rv.at[b, :, :, lanes], psem.at[pair + 1]),
            ))

    bar = pltpu.get_barrier_semaphore()
    greet = [member(g, (mine[g] + k) % 8) for g in range(3) for k in range(1, 8)]
    greet += [dev((x + dx) % 4, (y + dy) % 4, z, c) for dy in range(1, 4) for dx in range(1, 4)]
    for to in greet:
        pl.semaphore_signal(bar, 1, device_id=to, device_id_type=MESH)
    lane8 = lax.broadcasted_iota(jnp.int32, (8, 128), 1)
    momv[...] = jnp.where(lane8 == 0, mom[0], mom[1])
    for g in range(3):
        moml[g, mine[g]] = momv[...]
    kacc[...] = jnp.zeros_like(kacc)
    pl.semaphore_wait(bar, len(greet))

    mom_out = []
    for g in range(3):
        for k in range(1, 8):
            mom_out.append(copy_to(
                momv, moml.at[g, mine[g]], msend.at[g, k - 1], mrecv.at[g, k - 1], member(g, (mine[g] + k) % 8)
            ))

    trial_out = []
    for k in range(1, 16):
        trial_out.append(copy_to(trial, xr.at[kc], xsend.at[k - 1], xrecv.at[k - 1], (kr, (kc + k) % 16)))
    for k in range(1, 8):
        trial_out.append(copy_to(trial, xc.at[kr], xsend.at[14 + k], xrecv.at[14 + k], ((kr + k) % 8, kc)))

    flow = {}

    def b_copy(u, i, src, dst, to):
        return copy_to(src, dst, bsend.at[u, i], brecv.at[u, i], to)

    def s0(u):
        own_b[u].wait()
        own = ag_b[u].at[y, x]
        to = (to_x, to_y)[u % 2]
        flow[u, 0] = go([b_copy(u, i, own, own, to[i]) for i in range(2)])

    def s1(u):
        for cp in flow[u, 0]:
            cp.wait_recv()
        if u % 2 == 0:
            a, b, to = ag_b[u].at[y, xm, 0:8], ag_b[u].at[y, xp, 8:16], to_x
        else:
            a, b, to = ag_b[u].at[ym, x, 0:8], ag_b[u].at[yp, x, 8:16], to_y
        flow[u, 1] = go([b_copy(u, 2, a, a, to[0]), b_copy(u, 3, b, b, to[1])])

    def s2(u):
        for cp in flow[u, 1]:
            cp.wait_recv()
        line, to = (ag_b[u].at[y], to_y) if u % 2 == 0 else (ag_b[u].at[:, x], to_x)
        flow[u, 2] = go([b_copy(u, 4, line, line, to[0]), b_copy(u, 5, line, line, to[1])])

    def s3(u):
        for cp in flow[u, 2]:
            cp.wait_recv()
        if u % 2 == 0:
            a, b, to = ag_b[u].at[ym, 0:2], ag_b[u].at[yp, 2:4], to_y
        else:
            a, b, to = ag_b[u].at[0:2, xm], ag_b[u].at[2:4, xp], to_x
        flow[u, 3] = go([b_copy(u, 6, a, a, to[0]), b_copy(u, 7, b, b, to[1])])

    arrive_b = [[] for _ in range(NU)]
    arrive_d = [[] for _ in range(NC)]

    def s4(u):
        for cp in flow[u, 3]:
            cp.wait_recv()
        me = mine[0]
        for k in range(1, 8):
            d = (me + k) % 8
            for s in range(2):
                st_b[u, k - 1, s] = ag_b[u][:, :, moms[0, d, 0, s]].reshape(16, 16, 128)
            arrive_b[u] += go([copy_to(
                st_b.at[u, k - 1], land_b.at[me, u], asend.at[u, k - 1], arecv.at[u, k - 1], member(0, d)
            )])
        for s in range(2):
            land_b[me, u, s] = ag_b[u][:, :, moms[0, me, 0, s]].reshape(16, 16, 128)

    def t0(h):
        for p, (ag, pos, to) in enumerate(((ag_1, y, to_y), (ag_2, x, to_x))):
            own_d[p][h].wait()
            own = ag[h].at[pos]
            flow[p, h, 0] = go([copy_to(own, own, dsend.at[p, h, i], drecv.at[p, h, i], to[i]) for i in range(2)])

    def t1(h):
        for p, (ag, m, q, to) in enumerate(((ag_1, ym, yp, to_y), (ag_2, xm, xp, to_x))):
            for cp in flow[p, h, 0]:
                cp.wait_recv()
            a, b = ag[h].at[m, 0:8], ag[h].at[q, 8:16]
            flow[p, h, 1] = go([
                copy_to(a, a, dsend.at[p, h, 2], drecv.at[p, h, 2], to[0]),
                copy_to(b, b, dsend.at[p, h, 3], drecv.at[p, h, 3], to[1]),
            ])

    def t2(h):
        for p, (ag, land) in enumerate(((ag_1, land_1), (ag_2, land_2))):
            for cp in flow[p, h, 1]:
                cp.wait_recv()
            u = p * NC + h
            for stage in range(4):
                for cp in flow[u, stage]:
                    cp.wait_send()
                    left.add(id(cp))
            me = mine[1 + p]
            for k in range(1, 8):
                d = (me + k) % 8
                place = ag_b[u].at[(k - 1) // 2, pl.ds(2 * ((k - 1) % 2), 2)]
                for s in range(2):
                    place[s] = ag[h][:, moms[1 + p, d, 0, s]].reshape(16, 16, 128)
                arrive_d[h] += go([copy_to(
                    place, land.at[me, h], asend.at[NU + u, k - 1], arecv.at[NU + u, k - 1], member(1 + p, d)
                )])
            for s in range(2):
                land[me, h, s] = ag[h][:, moms[1 + p, me, 0, s]].reshape(16, 16, 128)

    def m0():
        for cp in mom_out:
            cp.wait()
        cp = pltpu.make_async_copy(moml, moms, lsem.at[NU + 2 * NC])
        cp.start()
        cp.wait()

    def pack(b):
        for half in range(2):
            for cp in dens_in[b * 2 + half]:
                cp.wait()

        @pl.loop(0, 16)
        def _(i):
            for half in range(2):
                lanes = pl.ds(half * 128, 128)
                a = rcd[b, i, :, lanes]
                v = rv[b, i, :, lanes]
                low = lax.broadcasted_iota(jnp.int32, (128, 128), 1) < 64
                rcd[b, i, :, lanes] = jnp.where(low, a, pltpu.roll(v, 64, 1))
                rv[b, i, :, lanes] = jnp.where(low, pltpu.roll(a, 64, 1), v)

    def multiply(load_w, load_c):
        def gather(b, val):
            for half in range(2):
                lanes = slice(half * 128, half * 128 + 128)
                kacc[b * 2 + half] += lax.dot_general(
                    load_c(b, lanes), val[:, lanes], (((0,), (0,)), ((), ())), preferred_element_type=F32
                )

        before = None
        for b in range(8):
            if b % 4 == 0:
                lhs = load_w(b // 4)
            val = jnp.dot(lhs, rv[b].reshape(2048, 256), preferred_element_type=F32).astype(BF)
            if before is not None:
                gather(b - 1, before)
            before = val
        gather(7, before)

    def c_step(t):
        for u in (2 * t, 2 * t + 1):
            for cp in arrive_b[u]:
                cp.wait_recv()

        def load_w(s):
            return jnp.concatenate(
                [land_b[:, 2 * t:2 * t + 2, s, j].reshape(256, 128) for j in range(16)], axis=1
            )

        def load_c(b, lanes):
            return rcd[b, 0:8, 32 * t:32 * t + 32, lanes].reshape(256, 128)

        multiply(load_w, load_c)

    def e_step(h):
        for cp in arrive_d[h]:
            cp.wait_recv()

        def load_w(s):
            parts = []
            for j in range(16):
                yy, xx = j // 4, j % 4
                parts.append(jnp.concatenate(
                    [land_1[xx * 2 + cc, h, s, 4 * yy:4 * yy + 4].reshape(64, 128) for cc in range(2)]
                    + [land_2[yy * 2 + cc, h, s, 4 * xx:4 * xx + 4].reshape(64, 128) for cc in range(2)],
                    axis=0,
                ))
            return jnp.concatenate(parts, axis=1)

        def load_c(b, lanes):
            part = slice((h % 2) * 64, (h % 2) * 64 + 64)
            return jnp.concatenate([rcd[b, 8 + 2 * i + h // 2, part, lanes] for i in range(4)], axis=0)

        multiply(load_w, load_c)

    def x_step():
        for cp in trial_out:
            cp.wait()
        xr[kc] = trial[...]
        xc[kr] = trial[...]
        low = lax.broadcasted_iota(jnp.int32, (8, 128), 1) < 64
        src = lax.broadcasted_iota(jnp.int32, (128, 1024), 0)
        dst = lax.broadcasted_iota(jnp.int32, (128, 1024), 1)
        n, p2, v, vv = dst // 128, (dst // 64) % 2, (dst // 8) % 8, dst % 8
        for land, size, pairs, table, band in ((xr, 16, rows, bc, v), (xc, 8, cols, br, vv)):
            xf[0:size * 2] = land[...].astype(F32).reshape(size * 2, 8, 128)
            spread = (src == p2 * 64 + band * 8 + n).astype(F32)
            for pp in range(16):
                first = xf[pairs[2 * pp]]
                second = xf[pairs[2 * pp + 1]]
                both = jnp.where(low, first, second)
                table[pp] = jnp.dot(both, spread, preferred_element_type=F32)

    def y_step():
        lane = lax.broadcasted_iota(jnp.int32, (1, 128), 1)
        for pp in range(16):
            for pairs, band, table, size in ((rows, (lane // 8) % 8, pick_r, 256), (cols, lane % 8, pick_c, 128)):
                p = 2 * pp
                place = jnp.where(lane < 64, pairs[p], pairs[p + 1])
                listed = jnp.where(lane < 64, p % 16, p % 16 + 1) < count[p // 16]
                key = jnp.where(listed, place * 8 + band, -1)
                at = lax.broadcasted_iota(jnp.int32, (size, 128), 0)
                table[pp] = (at == key).astype(F32).astype(BF)

    def finish():
        sum_r[...] = jnp.zeros_like(sum_r)
        sum_c[...] = jnp.zeros_like(sum_c)

        @pl.loop(0, 16)
        def _(pp):
            low = lax.broadcasted_iota(jnp.int32, (64, 128), 1) < 64
            kd[...] = jnp.where(low, kacc[pp, 0:64], kacc[pp, 64:128])
            by_row = [kd[pl.ds(i, 8, stride=8)] for i in range(8)]
            by_col = [kd[8 * i:8 * i + 8] for i in range(8)]
            for table, pieces, pick, total in ((br, by_row, pick_r, sum_r), (bc, by_col, pick_c, sum_c)):
                parts = []
                for n in range(8):
                    lanes = slice(n * 128, n * 128 + 128)
                    parts.append(sum(pieces[i] * table[pp, i:i + 1, lanes] for i in range(8)))
                whole = jnp.concatenate(parts, axis=0)
                high = whole.astype(BF)
                rest = (whole - high.astype(F32)).astype(BF)
                total[...] += lax.dot_general(
                    pick[pp], jnp.concatenate([high, rest], axis=0), (((1,), (1,)), ((), ())),
                    preferred_element_type=F32,
                )

        last = []
        for k in range(1, 16):
            d = (kc + k) % 16
            last.append(copy_to(
                sum_r.at[pl.ds(pl.multiple_of(d * 16, 16), 16)], land_r.at[kc],
                ysend.at[k - 1], yrecv.at[k - 1], (kr, d),
            ))
        for k in range(1, 8):
            d = (kr + k) % 8
            last.append(copy_to(
                sum_c.at[pl.ds(pl.multiple_of(d * 16, 16), 16)], land_c.at[kr],
                ysend.at[14 + k], yrecv.at[14 + k], (d, kc),
            ))
        for cp in last:
            cp.start()
        land_r[kc] = sum_r[pl.ds(pl.multiple_of(kc * 16, 16), 16)]
        land_c[kr] = sum_c[pl.ds(pl.multiple_of(kr * 16, 16), 16)]
        for cp in last:
            cp.wait()
        total = land_r[0] + land_c[0]
        for i in range(1, 16):
            total += land_r[i]
        for i in range(1, 8):
            total += land_c[i]
        out[...] = total

    for cp in mom_out:
        cp.start()
    started = False
    steps = {"S0": s0, "S1": s1, "S2": s2, "S3": s3, "S4": s4, "T0": t0, "T1": t1, "T2": t2}
    for step in SEQ:
        i = int(step[-1])
        if step[0] == "S":
            steps[step[:2]](2 * i)
            steps[step[:2]](2 * i + 1)
        elif step[0] == "T":
            steps[step[:2]](i)
        elif step[0] == "M":
            m0()
            for cp in trial_out:
                cp.start()
        elif step[0] == "P":
            pack(i)
        elif step[0] == "X":
            x_step()
        elif step[0] == "Y":
            y_step()
        elif step[0] == "C":
            c_step(i)
        elif step[0] == "E":
            e_step(i)
    finish()
    for cp in sent:
        if id(cp) not in left:
            cp.wait_send()


def body(trial, screened, density, pair_rows, pair_cols, slot_momentum, slot_count):
    half = trial.reshape(16, 64)
    doubled = jnp.concatenate([half, half], axis=1)
    smem = pl.BlockSpec(memory_space=pltpu.SMEM)
    anywhere = pl.BlockSpec(memory_space=pl.ANY)
    vmem = pl.BlockSpec(memory_space=pltpu.VMEM)
    dma = pltpu.SemaphoreType.DMA
    total = pl.pallas_call(
        kernel,
        out_shape=jax.ShapeDtypeStruct((16, 128), F32),
        in_specs=[anywhere, anywhere, smem, smem, smem, smem, vmem],
        out_specs=vmem,
        scratch_shapes=[
            pltpu.VMEM((8, 128), jnp.int32),
            pltpu.VMEM((3, 8, 8, 128), jnp.int32),
            pltpu.SMEM((3, 8, 8, 128), jnp.int32),
            *[pltpu.VMEM((4, 4, 16, 16, 128), BF)] * NU,
            *[pltpu.VMEM((4, 16, RC, 128), BF)] * (2 * NC),
            pltpu.VMEM((NU, 7, 2, 16, 16, 128), BF),
            pltpu.VMEM((8, NU, 2, 16, 16, 128), BF),
            pltpu.VMEM((8, NC, 2, 16, 16, 128), BF),
            pltpu.VMEM((8, NC, 2, 16, 16, 128), BF),
            pltpu.VMEM((8, 16, 128, 256), BF),
            pltpu.VMEM((8, 16, 128, 256), BF),
            pltpu.VMEM((16, 128, 128), F32),
            pltpu.VMEM((16, 16, 128), BF),
            pltpu.VMEM((8, 16, 128), BF),
            pltpu.VMEM((32, 8, 128), F32),
            pltpu.VMEM((16, 8, 1024), F32),
            pltpu.VMEM((16, 8, 1024), F32),
            pltpu.VMEM((16, 256, 128), BF),
            pltpu.VMEM((16, 128, 128), BF),
            pltpu.VMEM((64, 128), F32),
            pltpu.VMEM((256, 128), F32),
            pltpu.VMEM((128, 128), F32),
            pltpu.VMEM((16, 16, 128), F32),
            pltpu.VMEM((8, 16, 128), F32),
            dma((3, 7)), dma((3, 7)), dma((NU, 8)), dma((NU, 8)), dma((2, NC, 4)), dma((2, NC, 4)),
            dma((NU + 2 * NC, 7)), dma((NU + 2 * NC, 7)), dma((22,)), dma((22,)), dma((22,)), dma((22,)),
            dma((NU + 2 * NC + 1,)), dma((32,)),
        ],
        compiler_params=pltpu.CompilerParams(
            collective_id=0, has_side_effects=True, vmem_limit_bytes=62 * 2**20
        ),
    )(
        screened, density.reshape(density.shape[0], 16, 128, 128),
        slot_momentum, slot_count, pair_rows, pair_cols, doubled,
    )
    total = total.reshape(2, 8, 2, 8, 8)
    total = total[:, :, 0] + total[:, :, 1]
    return total.transpose(0, 3, 1, 2).reshape(2, 512)


def solution(mesh):
    return jax.shard_map(
        body,
        mesh=mesh,
        in_specs=(
            P(("kr", "kc"), None),
            P(None, None, "kc"),
            P(("kr", "kc"), None, None),
            P(("kr", "kc")),
            P(("kr", "kc")),
            P(("kr", "kc")),
            P(("kr", "kc")),
        ),
        out_specs=P(("kr", "kc"), None),
        check_vma=False,
    )
```

```python
import functools

import jax
import jax.numpy as jnp
from jax import lax
from jax.experimental import pallas as pl
from jax.experimental.pallas import tpu as pltpu
from jax.sharding import PartitionSpec as P

MESH = pl.DeviceIdType.MESH
F32 = jnp.float32
BF = jnp.bfloat16
NU = 8
NC = 4
RC = 64
PLANE_ROWS = 1024

SEQ = (
    "S00", "T000", "S02", "S05", "S01", "S03", "L0", "N0", "S06", "S10", "S07", "S04", "T012", "P0",
    "S12", "S11", "S15", "T010", "S20", "S21", "S13", "T100", "S30", "T001", "S16", "T110",
    "M0", "S22", "S17", "S31", "T011", "S14", "S23", "S40", "T101", "S41", "P5", "P7",
    "P6", "S32", "S24", "P1", "S27", "P2", "S25", "P4", "S33", "T210", "S42", "S34",
    "T013", "S35", "P3", "T200", "T003", "S26", "S43", "S45", "X0", "Y0", "T103", "T111",
    "T113", "T002", "S44", "T112", "S36", "S37", "T201", "T211", "C0", "T102", "T213", "T203",
    "E0", "S47", "S46", "C1", "E1", "T202", "C2", "T212", "E3", "C3", "E2",
)


def kernel(w, dens, mom, count, rows, cols, trial, out, momv, moml, moms, *scratch):
    ag_b, ag_1, ag_2 = scratch[:NU], scratch[NU:NU + NC], scratch[NU + NC:NU + 2 * NC]
    (
        st_b, land_b, land_1, land_2,
        rv, rcd, kacc, xr, xc, xf, br, bc, pick_r, pick_c, kd, sum_r, sum_c, land_r, land_c,
        msend, mrecv, bsend, brecv, dsend, drecv, asend, arecv, xsend, xrecv, ysend, yrecv, lsem, psem,
    ) = scratch[NU + 2 * NC:]
    kr = lax.axis_index("kr")
    kc = lax.axis_index("kc")
    z, c, y, x = kr // 2, kr % 2, kc // 4, kc % 4

    def dev(x_, y_, z_, c_):
        return (z_ * 2 + c_, y_ * 4 + x_)

    def member(g, d):
        a, cc = d // 2, d % 2
        return (dev(x, y, a, cc), dev(a, y, z, cc), dev(x, a, z, cc))[g]

    mine = (z * 2 + c, x * 2 + c, y * 2 + c)
    xp, xm, yp, ym = (x + 1) % 4, (x + 3) % 4, (y + 1) % 4, (y + 3) % 4
    to_x = (dev(xp, y, z, c), dev(xm, y, z, c))
    to_y = (dev(x, yp, z, c), dev(x, ym, z, c))

    def copy_to(src, dst, ss, rs, to):
        return pltpu.make_async_remote_copy(
            src_ref=src, dst_ref=dst, send_sem=ss, recv_sem=rs, device_id=to, device_id_type=MESH
        )

    sent = []
    left = set()

    def go(copies):
        for cp in copies:
            cp.start()
            sent.append(cp)
        return copies

    bar = pltpu.get_barrier_semaphore()
    greet = [member(g, (mine[g] + k) % 8) for g in range(3) for k in range(1, 8)]
    greet += [dev((x + dx) % 4, (y + dy) % 4, z, c) for dy in range(1, 4) for dx in range(1, 4)]
    for to in greet:
        pl.semaphore_signal(bar, 1, device_id=to, device_id_type=MESH)

    def local(src, dst, sem):
        cp = pltpu.make_async_copy(src, dst, sem)
        cp.start()
        return cp

    def rows_b(u):
        return pl.ds(pl.multiple_of(kr * (NU * 16) + u * 16, 16), 16)

    def rows_d(p, h):
        return pl.ds(pl.multiple_of(PLANE_ROWS + p * 512 + c * 256 + h * RC, 16), RC)

    own_b = [local(w.at[:, rows_b(u)], ag_b[u].at[y, x], lsem.at[u]) for u in range(NU)]
    own_d = [
        [local(w.at[:, rows_d(0, h)], ag_1[h].at[y], lsem.at[NU + h]) for h in range(NC)],
        [local(w.at[:, rows_d(1, h)], ag_2[h].at[x], lsem.at[NU + NC + h]) for h in range(NC)],
    ]
    dens_in = []

    def load():
        for b in range(8):
            for half in range(2):
                pair = (b * 2 + half) * 2
                lanes = pl.ds(half * 128, 128)
                dens_in.append((
                    local(dens.at[pair], rcd.at[b, :, :, lanes], psem.at[pair]),
                    local(dens.at[pair + 1], rv.at[b, :, :, lanes], psem.at[pair + 1]),
                ))

    lane8 = lax.broadcasted_iota(jnp.int32, (8, 128), 1)
    momv[...] = jnp.where(lane8 == 0, mom[0], mom[1])
    for g in range(3):
        moml[g, mine[g]] = momv[...]
    kacc[...] = jnp.zeros_like(kacc)
    pl.semaphore_wait(bar, len(greet))

    mom_out = []
    for g in range(3):
        for k in range(1, 8):
            mom_out.append(copy_to(
                momv, moml.at[g, mine[g]], msend.at[g, k - 1], mrecv.at[g, k - 1], member(g, (mine[g] + k) % 8)
            ))

    trial_out = []
    for k in range(1, 16):
        trial_out.append(copy_to(trial, xr.at[kc], xsend.at[k - 1], xrecv.at[k - 1], (kr, (kc + k) % 16)))
    for k in range(1, 8):
        trial_out.append(copy_to(trial, xc.at[kr], xsend.at[14 + k], xrecv.at[14 + k], ((kr + k) % 8, kc)))

    flow = {}

    def b_copy(u, i, src, dst, to):
        return copy_to(src, dst, bsend.at[u, i], brecv.at[u, i], to)

    def s0(u):
        own_b[u].wait()
        own = ag_b[u].at[y, x]
        to = (to_x, to_y)[u % 2]
        flow[u, 0] = go([b_copy(u, i, own, own, to[i]) for i in range(2)])

    def s1(u):
        for cp in flow[u, 0]:
            cp.wait_recv()
        if u % 2 == 0:
            a, b, to = ag_b[u].at[y, xm, 0:8], ag_b[u].at[y, xp, 8:16], to_x
        else:
            a, b, to = ag_b[u].at[ym, x, 0:8], ag_b[u].at[yp, x, 8:16], to_y
        flow[u, 1] = go([b_copy(u, 2, a, a, to[0]), b_copy(u, 3, b, b, to[1])])

    def s2(u):
        for cp in flow[u, 1]:
            cp.wait_recv()
        line, to = (ag_b[u].at[y], to_y) if u % 2 == 0 else (ag_b[u].at[:, x], to_x)
        flow[u, 2] = go([b_copy(u, 4, line, line, to[0]), b_copy(u, 5, line, line, to[1])])

    def s3(u):
        for cp in flow[u, 2]:
            cp.wait_recv()
        if u % 2 == 0:
            a, b, to = ag_b[u].at[ym, 0:2], ag_b[u].at[yp, 2:4], to_y
        else:
            a, b, to = ag_b[u].at[0:2, xm], ag_b[u].at[2:4, xp], to_x
        flow[u, 3] = go([b_copy(u, 6, a, a, to[0]), b_copy(u, 7, b, b, to[1])])

    free_units = []
    arrive_b = [[] for _ in range(NU)]
    arrive_d = [[] for _ in range(NC)]

    def s4(u):
        for cp in flow[u, 3]:
            cp.wait_recv()
        me = mine[0]
        for k in range(1, 8):
            d = (me + k) % 8
            for s in range(2):
                st_b[u, k - 1, s] = ag_b[u][:, :, moms[0, d, 0, s]].reshape(16, 16, 128)
            arrive_b[u] += go([copy_to(
                st_b.at[u, k - 1], land_b.at[me, u], asend.at[u, k - 1], arecv.at[u, k - 1], member(0, d)
            )])
        for s in range(2):
            land_b[me, u, s] = ag_b[u][:, :, moms[0, me, 0, s]].reshape(16, 16, 128)
        free_units.append(u)

    def t0(p, h):
        ag, pos, to = ((ag_1, y, to_y), (ag_2, x, to_x))[p]
        own_d[p][h].wait()
        own = ag[h].at[pos]
        flow[p, h, 0] = go([copy_to(own, own, dsend.at[p, h, i], drecv.at[p, h, i], to[i]) for i in range(2)])

    def t1(p, h):
        ag, m, q, to = ((ag_1, ym, yp, to_y), (ag_2, xm, xp, to_x))[p]
        for cp in flow[p, h, 0]:
            cp.wait_recv()
        a, b = ag[h].at[m, 0:8], ag[h].at[q, 8:16]
        flow[p, h, 1] = go([
            copy_to(a, a, dsend.at[p, h, 2], drecv.at[p, h, 2], to[0]),
            copy_to(b, b, dsend.at[p, h, 3], drecv.at[p, h, 3], to[1]),
        ])

    def t2(p, h):
        ag, land = ((ag_1, land_1), (ag_2, land_2))[p]
        for cp in flow[p, h, 1]:
            cp.wait_recv()
        u = free_units.pop(0)
        r = NU + p * NC + h
        for stage in range(4):
            for cp in flow[u, stage]:
                cp.wait_send()
                left.add(id(cp))
        me = mine[1 + p]
        for k in range(1, 8):
            d = (me + k) % 8
            place = ag_b[u].at[(k - 1) // 2, pl.ds(2 * ((k - 1) % 2), 2)]
            for s in range(2):
                place[s] = ag[h][:, moms[1 + p, d, 0, s]].reshape(16, 16, 128)
            arrive_d[h] += go([copy_to(
                place, land.at[me, h], asend.at[r, k - 1], arecv.at[r, k - 1], member(1 + p, d)
            )])
        for s in range(2):
            land[me, h, s] = ag[h][:, moms[1 + p, me, 0, s]].reshape(16, 16, 128)

    def m0():
        for cp in mom_out:
            cp.wait()
        cp = pltpu.make_async_copy(moml, moms, lsem.at[NU + 2 * NC])
        cp.start()
        cp.wait()

    def pack(b):
        for half in range(2):
            for cp in dens_in[b * 2 + half]:
                cp.wait()

        @pl.loop(0, 4)
        def _(i):
            part = pl.ds(i * 4, 4)
            for half in range(2):
                lanes = pl.ds(half * 128, 128)
                a = rcd[b, part, :, lanes].reshape(512, 128)
                v = pltpu.roll(rv[b, part, :, lanes].reshape(512, 128), 64, 1)
                low = lax.broadcasted_iota(jnp.int32, (512, 128), 1) < 64
                rcd[b, part, :, lanes] = jnp.where(low, a, v).reshape(4, 128, 128)
                rv[b, part, :, lanes] = jnp.where(low, v, a).reshape(4, 128, 128)

    def multiply(load_w, load_c):
        def gather(b, val):
            for half in range(2):
                lanes = slice(half * 128, half * 128 + 128)
                kacc[b * 2 + half] += lax.dot_general(
                    load_c(b, lanes), val[:, lanes], (((0,), (0,)), ((), ())), preferred_element_type=F32
                )

        @pl.loop(0, 2)
        def _(s):
            lhs = load_w(s)
            before = None
            for i in range(4):
                b = s * 4 + i
                val = jnp.dot(lhs, rv[b].reshape(2048, 256), preferred_element_type=F32).astype(BF)
                if before is not None:
                    gather(b - 1, before)
                before = val
            gather(s * 4 + 3, before)

    def c_step(t):
        for u in (2 * t, 2 * t + 1):
            for cp in arrive_b[u]:
                cp.wait_recv()

        def load_w(s):
            return jnp.concatenate(
                [land_b[:, 2 * t:2 * t + 2, s, j].reshape(256, 128) for j in range(16)], axis=1
            )

        def load_c(b, lanes):
            return rcd[b, 0:8, 32 * t:32 * t + 32, lanes].reshape(256, 128)

        multiply(load_w, load_c)

    def e_step(h):
        for cp in arrive_d[h]:
            cp.wait_recv()

        def load_w(s):
            parts = []
            for j in range(16):
                yy, xx = j // 4, j % 4
                parts.append(jnp.concatenate(
                    [land_1[xx * 2 + cc, h, s, 4 * yy:4 * yy + 4].reshape(64, 128) for cc in range(2)]
                    + [land_2[yy * 2 + cc, h, s, 4 * xx:4 * xx + 4].reshape(64, 128) for cc in range(2)],
                    axis=0,
                ))
            return jnp.concatenate(parts, axis=1)

        def load_c(b, lanes):
            part = slice((h % 2) * 64, (h % 2) * 64 + 64)
            return jnp.concatenate([rcd[b, 8 + 2 * i + h // 2, part, lanes] for i in range(4)], axis=0)

        multiply(load_w, load_c)

    def x_step():
        for cp in trial_out:
            cp.wait()
        xr[kc] = trial[...]
        xc[kr] = trial[...]
        low = lax.broadcasted_iota(jnp.int32, (8, 128), 1) < 64
        src = lax.broadcasted_iota(jnp.int32, (128, 1024), 0)
        dst = lax.broadcasted_iota(jnp.int32, (128, 1024), 1)
        n, p2, v, vv = dst // 128, (dst // 64) % 2, (dst // 8) % 8, dst % 8
        for land, size, pairs, table, band in ((xr, 16, rows, bc, v), (xc, 8, cols, br, vv)):
            xf[0:size * 2] = land[...].astype(F32).reshape(size * 2, 8, 128)
            spread = (src == p2 * 64 + band * 8 + n).astype(F32)

            @pl.loop(0, 4)
            def _(g):
                both = [
                    jnp.where(low, xf[pairs[8 * g + 2 * j + 1]], xf[pairs[8 * g + 2 * j]]) for j in range(4)
                ]
                wide = jnp.dot(jnp.concatenate(both, axis=0), spread, preferred_element_type=F32)
                table[pl.ds(g * 4, 4)] = wide.reshape(4, 8, 1024)

    def y_step():
        lane = lax.broadcasted_iota(jnp.int32, (1, 128), 1)

        @pl.loop(0, 16)
        def _(pp):
            p = 2 * pp
            listed = jnp.where(lane < 64, (p + 1) % 16, p % 16) < count[pp // 8]
            for pairs, band, table, size in ((rows, (lane // 8) % 8, pick_r, 256), (cols, lane % 8, pick_c, 128)):
                place = jnp.where(lane < 64, pairs[p + 1], pairs[p])
                key = jnp.where(listed, place * 8 + band, -1)
                at = lax.broadcasted_iota(jnp.int32, (size, 128), 0)
                table[pp] = (at == key).astype(F32).astype(BF)

    def finish():
        sum_r[...] = jnp.zeros_like(sum_r)
        sum_c[...] = jnp.zeros_like(sum_c)

        def apply(pp, slot):
            low = lax.broadcasted_iota(jnp.int32, (64, 128), 1) < 64
            kd[slot] = jnp.where(low, kacc[pp, 64:128], kacc[pp, 0:64])
            by_row = [kd[slot, pl.ds(i, 8, stride=8)] for i in range(8)]
            by_col = [kd[slot, 8 * i:8 * i + 8] for i in range(8)]
            for table, pieces in ((br, by_row), (bc, by_col)):
                parts = []
                for n in range(8):
                    lanes = slice(n * 128, n * 128 + 128)
                    parts.append(sum(pieces[i] * table[pp, i:i + 1, lanes] for i in range(8)))
                whole = jnp.concatenate(parts, axis=0)
                high = whole.astype(BF)
                rest = (whole - high.astype(F32)).astype(BF)
                yield jnp.concatenate([high, rest], axis=0)

        @pl.loop(0, 4)
        def _(g):
            both = [tuple(apply(g * 4 + j, j)) for j in range(4)]
            for i, (pick, total) in enumerate(((pick_r, sum_r), (pick_c, sum_c))):
                total[...] += lax.dot_general(
                    jnp.concatenate([pick[g * 4 + j] for j in range(4)], axis=1),
                    jnp.concatenate([pair[i] for pair in both], axis=1),
                    (((1,), (1,)), ((), ())), preferred_element_type=F32,
                )

        last = []
        for k in range(1, 16):
            d = (kc + k) % 16
            last.append(copy_to(
                sum_r.at[pl.ds(pl.multiple_of(d * 16, 16), 16)], land_r.at[kc],
                ysend.at[k - 1], yrecv.at[k - 1], (kr, d),
            ))
        for k in range(1, 8):
            d = (kr + k) % 8
            last.append(copy_to(
                sum_c.at[pl.ds(pl.multiple_of(d * 16, 16), 16)], land_c.at[kr],
                ysend.at[14 + k], yrecv.at[14 + k], (d, kc),
            ))
        for cp in last:
            cp.start()
        land_r[kc] = sum_r[pl.ds(pl.multiple_of(kc * 16, 16), 16)]
        land_c[kr] = sum_c[pl.ds(pl.multiple_of(kr * 16, 16), 16)]
        for cp in last:
            cp.wait()
        total = land_r[0] + land_c[0]
        for i in range(1, 16):
            total += land_r[i]
        for i in range(1, 8):
            total += land_c[i]
        out[...] = total

    steps = {"S0": s0, "S1": s1, "S2": s2, "S3": s3, "S4": s4, "T0": t0, "T1": t1, "T2": t2}
    for step in SEQ:
        i = int(step[-1])
        if step[0] == "S":
            steps[step[:2]](i)
        elif step[0] == "T":
            steps[step[:2]](int(step[2]), i)
        elif step[0] == "L":
            load()
        elif step[0] == "N":
            for cp in mom_out:
                cp.start()
        elif step[0] == "M":
            m0()
            for cp in trial_out:
                cp.start()
        elif step[0] == "P":
            pack(i)
        elif step[0] == "X":
            x_step()
        elif step[0] == "Y":
            y_step()
        elif step[0] == "C":
            c_step(i)
        elif step[0] == "E":
            e_step(i)
    finish()
    for cp in sent:
        if id(cp) not in left:
            cp.wait_send()


def body(trial, screened, density, pair_rows, pair_cols, slot_momentum, slot_count):
    half = trial.reshape(16, 64)
    doubled = jnp.concatenate([half, half], axis=1)
    smem = pl.BlockSpec(memory_space=pltpu.SMEM)
    anywhere = pl.BlockSpec(memory_space=pl.ANY)
    vmem = pl.BlockSpec(memory_space=pltpu.VMEM)
    dma = pltpu.SemaphoreType.DMA
    total = pl.pallas_call(
        kernel,
        out_shape=jax.ShapeDtypeStruct((16, 128), F32),
        in_specs=[anywhere, anywhere, smem, smem, smem, smem, vmem],
        out_specs=vmem,
        scratch_shapes=[
            pltpu.VMEM((8, 128), jnp.int32),
            pltpu.VMEM((3, 8, 8, 128), jnp.int32),
            pltpu.SMEM((3, 8, 8, 128), jnp.int32),
            *[pltpu.VMEM((4, 4, 16, 16, 128), BF)] * NU,
            *[pltpu.VMEM((4, 16, RC, 128), BF)] * (2 * NC),
            pltpu.VMEM((NU, 7, 2, 16, 16, 128), BF),
            pltpu.VMEM((8, NU, 2, 16, 16, 128), BF),
            pltpu.VMEM((8, NC, 2, 16, 16, 128), BF),
            pltpu.VMEM((8, NC, 2, 16, 16, 128), BF),
            pltpu.VMEM((8, 16, 128, 256), BF),
            pltpu.VMEM((8, 16, 128, 256), BF),
            pltpu.VMEM((16, 128, 128), F32),
            pltpu.VMEM((16, 16, 128), BF),
            pltpu.VMEM((8, 16, 128), BF),
            pltpu.VMEM((32, 8, 128), F32),
            pltpu.VMEM((16, 8, 1024), F32),
            pltpu.VMEM((16, 8, 1024), F32),
            pltpu.VMEM((16, 256, 128), BF),
            pltpu.VMEM((16, 128, 128), BF),
            pltpu.VMEM((4, 64, 128), F32),
            pltpu.VMEM((256, 128), F32),
            pltpu.VMEM((128, 128), F32),
            pltpu.VMEM((16, 16, 128), F32),
            pltpu.VMEM((8, 16, 128), F32),
            dma((3, 7)), dma((3, 7)), dma((NU, 8)), dma((NU, 8)), dma((2, NC, 4)), dma((2, NC, 4)),
            dma((NU + 2 * NC, 7)), dma((NU + 2 * NC, 7)), dma((22,)), dma((22,)), dma((22,)), dma((22,)),
            dma((NU + 2 * NC + 1,)), dma((32,)),
        ],
        compiler_params=pltpu.CompilerParams(
            collective_id=0, has_side_effects=True, vmem_limit_bytes=62 * 2**20
        ),
    )(
        screened, density.reshape(density.shape[0], 16, 128, 128),
        slot_momentum, slot_count, pair_rows, pair_cols, doubled,
    )
    total = total.reshape(2, 8, 2, 8, 8)
    total = total[:, :, 0] + total[:, :, 1]
    return total.transpose(0, 3, 1, 2).reshape(2, 512)


def solution(mesh):
    return jax.shard_map(
        body,
        mesh=mesh,
        in_specs=(
            P(("kr", "kc"), None),
            P(None, None, "kc"),
            P(("kr", "kc"), None, None),
            P(("kr", "kc")),
            P(("kr", "kc")),
            P(("kr", "kc")),
            P(("kr", "kc")),
        ),
        out_specs=P(("kr", "kc"), None),
        check_vma=False,
    )
```

```python
import functools

import jax
import jax.numpy as jnp
from jax import lax
from jax.experimental import pallas as pl
from jax.experimental.pallas import tpu as pltpu
from jax.sharding import PartitionSpec as P

MESH = pl.DeviceIdType.MESH
F32 = jnp.float32
BF = jnp.bfloat16
NCON = 8
NU = 8
NC = 4
RC = 64
PLANE_ROWS = 1024

SEQ = (
    "S00", "T000", "S02", "S05", "S01", "S03", "L0", "N0", "S06", "S10", "S07", "S04", "T012", "P0",
    "S12", "S11", "S15", "T010", "S20", "S21", "S13", "T100", "S30", "T001", "S16", "T110",
    "M0", "S22", "S17", "S31", "T011", "S14", "S23", "S40", "T101", "S41", "P5", "P7",
    "P6", "S32", "S24", "P1", "S27", "P2", "S25", "P4", "S33", "T210", "S42", "S34",
    "T013", "S35", "P3", "T200", "T003", "S26", "S43", "S45", "X0", "Y0", "T103", "T111",
    "T113", "T002", "S44", "T112", "S36", "S37", "T201", "T211", "C0", "T102", "T213", "T203",
    "E0", "S47", "S46", "C1", "E1", "T202", "C2", "T212", "E3", "C3", "E2",
)


def kernel(w, dens, mom, count, rows, cols, trial_in, out, trial, tf, place, momv, moml, moms, *scratch):
    ag_b, ag_1, ag_2 = scratch[:NU], scratch[NU:NU + NC], scratch[NU + NC:NU + 2 * NC]
    (
        st_b, land_b, land_1, land_2,
        rv, rcd, kacc, xr, xc, xf, br, bc, pick_r, pick_c, kd, sum_r, sum_c, land_r, land_c,
        msend, mrecv, bsend, brecv, dsend, drecv, asend, arecv, xsend, xrecv, ysend, yrecv, lsem, psem,
    ) = scratch[NU + 2 * NC:]
    kr = lax.axis_index("kr")
    kc = lax.axis_index("kc")
    z, c, y, x = kr // 2, kr % 2, kc // 4, kc % 4

    def dev(x_, y_, z_, c_):
        return (z_ * 2 + c_, y_ * 4 + x_)

    def member(g, d):
        a, cc = d // 2, d % 2
        return (dev(x, y, a, cc), dev(a, y, z, cc), dev(x, a, z, cc))[g]

    mine = (z * 2 + c, x * 2 + c, y * 2 + c)
    xp, xm, yp, ym = (x + 1) % 4, (x + 3) % 4, (y + 1) % 4, (y + 3) % 4
    to_x = (dev(xp, y, z, c), dev(xm, y, z, c))
    to_y = (dev(x, yp, z, c), dev(x, ym, z, c))

    def copy_to(src, dst, ss, rs, to):
        return pltpu.make_async_remote_copy(
            src_ref=src, dst_ref=dst, send_sem=ss, recv_sem=rs, device_id=to, device_id_type=MESH
        )

    sent = []
    left = set()

    def go(copies):
        for cp in copies:
            cp.start()
            sent.append(cp)
        return copies

    bar = pltpu.get_barrier_semaphore()
    greet = [member(g, (mine[g] + k) % 8) for g in range(3) for k in range(1, 8)]
    greet += [dev((x + dx) % 4, (y + dy) % 4, z, c) for dy in range(1, 4) for dx in range(1, 4)]
    for to in greet:
        pl.semaphore_signal(bar, 1, device_id=to, device_id_type=MESH)

    def local(src, dst, sem):
        cp = pltpu.make_async_copy(src, dst, sem)
        cp.start()
        return cp

    def rows_b(u):
        return pl.ds(pl.multiple_of(kr * (NU * 16) + u * 16, 16), 16)

    def rows_d(p, h):
        return pl.ds(pl.multiple_of(PLANE_ROWS + p * 512 + c * 256 + h * RC, 16), RC)

    own_b = [local(w.at[:, rows_b(u)], ag_b[u].at[y, x], lsem.at[u]) for u in range(NU)]
    own_d = [
        [local(w.at[:, rows_d(0, h)], ag_1[h].at[y], lsem.at[NU + h]) for h in range(NC)],
        [local(w.at[:, rows_d(1, h)], ag_2[h].at[x], lsem.at[NU + NC + h]) for h in range(NC)],
    ]
    dens_in = []

    def load():
        for b in range(8):
            for half in range(2):
                pair = (b * 2 + half) * 2
                lanes = pl.ds(half * 128, 128)
                dens_in.append((
                    local(dens.at[pair], rcd.at[b, :, :, lanes], psem.at[pair]),
                    local(dens.at[pair + 1], rv.at[b, :, :, lanes], psem.at[pair + 1]),
                ))

    tf[...] = jnp.zeros_like(tf)
    vectors = trial_in[...].astype(F32)
    for k in range(2):
        for i in range(NCON):
            tf[k * 8 + i:k * 8 + i + 1, 0:64] = vectors[k:k + 1, i * 64:i * 64 + 64]
    low16 = lax.broadcasted_iota(jnp.int32, (16, 128), 1) < 64
    trial[...] = jnp.where(low16, tf[...], pltpu.roll(tf[...], 64, 1)).astype(BF)
    lane8 = lax.broadcasted_iota(jnp.int32, (8, 128), 1)
    momv[...] = jnp.where(lane8 == 0, mom[0], mom[1])
    for g in range(3):
        moml[g, mine[g]] = momv[...]
    kacc[...] = jnp.zeros_like(kacc)
    pl.semaphore_wait(bar, len(greet))

    mom_out = []
    for g in range(3):
        for k in range(1, 8):
            mom_out.append(copy_to(
                momv, moml.at[g, mine[g]], msend.at[g, k - 1], mrecv.at[g, k - 1], member(g, (mine[g] + k) % 8)
            ))

    trial_out = []
    for k in range(1, 16):
        trial_out.append(copy_to(trial, xr.at[kc], xsend.at[k - 1], xrecv.at[k - 1], (kr, (kc + k) % 16)))
    for k in range(1, 8):
        trial_out.append(copy_to(trial, xc.at[kr], xsend.at[14 + k], xrecv.at[14 + k], ((kr + k) % 8, kc)))

    flow = {}

    def b_copy(u, i, src, dst, to):
        return copy_to(src, dst, bsend.at[u, i], brecv.at[u, i], to)

    def s0(u):
        own_b[u].wait()
        own = ag_b[u].at[y, x]
        to = (to_x, to_y)[u % 2]
        flow[u, 0] = go([b_copy(u, i, own, own, to[i]) for i in range(2)])

    def s1(u):
        for cp in flow[u, 0]:
            cp.wait_recv()
        if u % 2 == 0:
            a, b, to = ag_b[u].at[y, xm, 0:8], ag_b[u].at[y, xp, 8:16], to_x
        else:
            a, b, to = ag_b[u].at[ym, x, 0:8], ag_b[u].at[yp, x, 8:16], to_y
        flow[u, 1] = go([b_copy(u, 2, a, a, to[0]), b_copy(u, 3, b, b, to[1])])

    def s2(u):
        for cp in flow[u, 1]:
            cp.wait_recv()
        line, to = (ag_b[u].at[y], to_y) if u % 2 == 0 else (ag_b[u].at[:, x], to_x)
        flow[u, 2] = go([b_copy(u, 4, line, line, to[0]), b_copy(u, 5, line, line, to[1])])

    def s3(u):
        for cp in flow[u, 2]:
            cp.wait_recv()
        if u % 2 == 0:
            a, b, to = ag_b[u].at[ym, 0:2], ag_b[u].at[yp, 2:4], to_y
        else:
            a, b, to = ag_b[u].at[0:2, xm], ag_b[u].at[2:4, xp], to_x
        flow[u, 3] = go([b_copy(u, 6, a, a, to[0]), b_copy(u, 7, b, b, to[1])])

    free_units = []
    arrive_b = [[] for _ in range(NU)]
    arrive_d = [[] for _ in range(NC)]

    def s4(u):
        for cp in flow[u, 3]:
            cp.wait_recv()
        me = mine[0]
        for k in range(1, 8):
            d = (me + k) % 8
            for s in range(2):
                st_b[u, k - 1, s] = ag_b[u][:, :, moms[0, d, 0, s]].reshape(16, 16, 128)
            arrive_b[u] += go([copy_to(
                st_b.at[u, k - 1], land_b.at[me, u], asend.at[u, k - 1], arecv.at[u, k - 1], member(0, d)
            )])
        for s in range(2):
            land_b[me, u, s] = ag_b[u][:, :, moms[0, me, 0, s]].reshape(16, 16, 128)
        free_units.append(u)

    def t0(p, h):
        ag, pos, to = ((ag_1, y, to_y), (ag_2, x, to_x))[p]
        own_d[p][h].wait()
        own = ag[h].at[pos]
        flow[p, h, 0] = go([copy_to(own, own, dsend.at[p, h, i], drecv.at[p, h, i], to[i]) for i in range(2)])

    def t1(p, h):
        ag, m, q, to = ((ag_1, ym, yp, to_y), (ag_2, xm, xp, to_x))[p]
        for cp in flow[p, h, 0]:
            cp.wait_recv()
        a, b = ag[h].at[m, 0:8], ag[h].at[q, 8:16]
        flow[p, h, 1] = go([
            copy_to(a, a, dsend.at[p, h, 2], drecv.at[p, h, 2], to[0]),
            copy_to(b, b, dsend.at[p, h, 3], drecv.at[p, h, 3], to[1]),
        ])

    def t2(p, h):
        ag, land = ((ag_1, land_1), (ag_2, land_2))[p]
        for cp in flow[p, h, 1]:
            cp.wait_recv()
        u = free_units.pop(0)
        r = NU + p * NC + h
        for stage in range(4):
            for cp in flow[u, stage]:
                cp.wait_send()
                left.add(id(cp))
        me = mine[1 + p]
        for k in range(1, 8):
            d = (me + k) % 8
            stage_at = ag_b[u].at[(k - 1) // 2, pl.ds(2 * ((k - 1) % 2), 2)]
            for s in range(2):
                stage_at[s] = ag[h][:, moms[1 + p, d, 0, s]].reshape(16, 16, 128)
            arrive_d[h] += go([copy_to(
                stage_at, land.at[me, h], asend.at[r, k - 1], arecv.at[r, k - 1], member(1 + p, d)
            )])
        for s in range(2):
            land[me, h, s] = ag[h][:, moms[1 + p, me, 0, s]].reshape(16, 16, 128)

    def m0():
        for cp in mom_out:
            cp.wait()
        cp = pltpu.make_async_copy(moml, moms, lsem.at[NU + 2 * NC])
        cp.start()
        cp.wait()

    def pack(b):
        for half in range(2):
            for cp in dens_in[b * 2 + half]:
                cp.wait()

        @pl.loop(0, 4)
        def _(i):
            part = pl.ds(i * 4, 4)
            for half in range(2):
                lanes = pl.ds(half * 128, 128)
                a = rcd[b, part, :, lanes].reshape(512, 128)
                v = pltpu.roll(rv[b, part, :, lanes].reshape(512, 128), 64, 1)
                low = lax.broadcasted_iota(jnp.int32, (512, 128), 1) < 64
                rcd[b, part, :, lanes] = jnp.where(low, a, v).reshape(4, 128, 128)
                rv[b, part, :, lanes] = jnp.where(low, v, a).reshape(4, 128, 128)

    def multiply(load_w, load_c):
        def gather(b, val):
            for half in range(2):
                lanes = slice(half * 128, half * 128 + 128)
                kacc[b * 2 + half] += lax.dot_general(
                    load_c(b, lanes), val[:, lanes], (((0,), (0,)), ((), ())), preferred_element_type=F32
                )

        @pl.loop(0, 2)
        def _(s):
            lhs = load_w(s)
            before = None
            for i in range(4):
                b = s * 4 + i
                val = jnp.dot(lhs, rv[b].reshape(2048, 256), preferred_element_type=F32).astype(BF)
                if before is not None:
                    gather(b - 1, before)
                before = val
            gather(s * 4 + 3, before)

    def c_step(t):
        for u in (2 * t, 2 * t + 1):
            for cp in arrive_b[u]:
                cp.wait_recv()

        def load_w(s):
            return jnp.concatenate(
                [land_b[:, 2 * t:2 * t + 2, s, j].reshape(256, 128) for j in range(16)], axis=1
            )

        def load_c(b, lanes):
            return rcd[b, 0:8, 32 * t:32 * t + 32, lanes].reshape(256, 128)

        multiply(load_w, load_c)

    def e_step(h):
        for cp in arrive_d[h]:
            cp.wait_recv()

        def load_w(s):
            parts = []
            for j in range(16):
                yy, xx = j // 4, j % 4
                parts.append(jnp.concatenate(
                    [land_1[xx * 2 + cc, h, s, 4 * yy:4 * yy + 4].reshape(64, 128) for cc in range(2)]
                    + [land_2[yy * 2 + cc, h, s, 4 * xx:4 * xx + 4].reshape(64, 128) for cc in range(2)],
                    axis=0,
                ))
            return jnp.concatenate(parts, axis=1)

        def load_c(b, lanes):
            part = slice((h % 2) * 64, (h % 2) * 64 + 64)
            return jnp.concatenate([rcd[b, 8 + 2 * i + h // 2, part, lanes] for i in range(4)], axis=0)

        multiply(load_w, load_c)

    def x_step():
        for cp in trial_out:
            cp.wait()
        xr[kc] = trial[...]
        xc[kr] = trial[...]
        src = lax.broadcasted_iota(jnp.int32, (128, 512), 0)
        dst = lax.broadcasted_iota(jnp.int32, (128, 512), 1)
        place[...] = ((src % 64) == (dst % 8) * 8 + dst // 64).astype(F32).astype(BF)
        low = lax.broadcasted_iota(jnp.int32, (8, 128), 1) < 64
        src = lax.broadcasted_iota(jnp.int32, (128, 1024), 0)
        dst = lax.broadcasted_iota(jnp.int32, (128, 1024), 1)
        n, p2, v, vv = dst // 128, (dst // 64) % 2, (dst // 8) % 8, dst % 8
        for land, size, pairs, table, band in ((xr, 16, rows, bc, v), (xc, 8, cols, br, vv)):
            xf[0:size * 2] = land[...].astype(F32).reshape(size * 2, 8, 128)
            spread = (src == p2 * 64 + band * 8 + n).astype(F32)

            @pl.loop(0, 4)
            def _(g):
                both = [
                    jnp.where(low, xf[pairs[8 * g + 2 * j + 1]], xf[pairs[8 * g + 2 * j]]) for j in range(4)
                ]
                wide = jnp.dot(jnp.concatenate(both, axis=0), spread, preferred_element_type=F32)
                table[pl.ds(g * 4, 4)] = wide.reshape(4, 8, 1024)

    def y_step():
        lane = lax.broadcasted_iota(jnp.int32, (1, 128), 1)

        @pl.loop(0, 16)
        def _(pp):
            p = 2 * pp
            listed = jnp.where(lane < 64, (p + 1) % 16, p % 16) < count[pp // 8]
            for pairs, band, table, size in ((rows, (lane // 8) % 8, pick_r, 256), (cols, lane % 8, pick_c, 128)):
                index = jnp.where(lane < 64, pairs[p + 1], pairs[p])
                key = jnp.where(listed, index * 8 + band, -1)
                at = lax.broadcasted_iota(jnp.int32, (size, 128), 0)
                table[pp] = (at == key).astype(F32).astype(BF)

    def finish():
        sum_r[...] = jnp.zeros_like(sum_r)
        sum_c[...] = jnp.zeros_like(sum_c)

        def apply(pp, slot):
            low = lax.broadcasted_iota(jnp.int32, (64, 128), 1) < 64
            kd[slot] = jnp.where(low, kacc[pp, 64:128], kacc[pp, 0:64])
            by_row = [kd[slot, pl.ds(i, 8, stride=8)] for i in range(8)]
            by_col = [kd[slot, 8 * i:8 * i + 8] for i in range(8)]
            for table, pieces in ((br, by_row), (bc, by_col)):
                parts = []
                for n in range(8):
                    lanes = slice(n * 128, n * 128 + 128)
                    parts.append(sum(pieces[i] * table[pp, i:i + 1, lanes] for i in range(8)))
                whole = jnp.concatenate(parts, axis=0)
                high = whole.astype(BF)
                rest = (whole - high.astype(F32)).astype(BF)
                yield jnp.concatenate([high, rest], axis=0)

        @pl.loop(0, 4)
        def _(g):
            both = [tuple(apply(g * 4 + j, j)) for j in range(4)]
            for i, (pick, total) in enumerate(((pick_r, sum_r), (pick_c, sum_c))):
                total[...] += lax.dot_general(
                    jnp.concatenate([pick[g * 4 + j] for j in range(4)], axis=1),
                    jnp.concatenate([pair[i] for pair in both], axis=1),
                    (((1,), (1,)), ((), ())), preferred_element_type=F32,
                )

        last = []
        for k in range(1, 16):
            d = (kc + k) % 16
            last.append(copy_to(
                sum_r.at[pl.ds(pl.multiple_of(d * 16, 16), 16)], land_r.at[kc],
                ysend.at[k - 1], yrecv.at[k - 1], (kr, d),
            ))
        for k in range(1, 8):
            d = (kr + k) % 8
            last.append(copy_to(
                sum_c.at[pl.ds(pl.multiple_of(d * 16, 16), 16)], land_c.at[kr],
                ysend.at[14 + k], yrecv.at[14 + k], (d, kc),
            ))
        for cp in last:
            cp.start()
        land_r[kc] = sum_r[pl.ds(pl.multiple_of(kc * 16, 16), 16)]
        land_c[kr] = sum_c[pl.ds(pl.multiple_of(kr * 16, 16), 16)]
        for cp in last:
            cp.wait()
        total = land_r[0] + land_c[0]
        for i in range(1, 16):
            total += land_r[i]
        for i in range(1, 8):
            total += land_c[i]
        parts = []
        for _ in range(3):
            parts.append(total.astype(BF))
            total = total - parts[-1].astype(F32)
        wide = jnp.dot(jnp.concatenate(parts, axis=0), place[...], preferred_element_type=F32)
        wide = wide[0:16] + wide[16:32] + wide[32:48]
        v = lax.broadcasted_iota(jnp.int32, (16, 512), 0) % 8
        wide = jnp.where(v == (lax.broadcasted_iota(jnp.int32, (16, 512), 1) // 8) % 8, wide, 0.0)
        for k in range(2):
            out[k:k + 1] = jnp.sum(wide[k * 8:k * 8 + 8], axis=0, keepdims=True)

    steps = {"S0": s0, "S1": s1, "S2": s2, "S3": s3, "S4": s4, "T0": t0, "T1": t1, "T2": t2}
    for step in SEQ:
        i = int(step[-1])
        if step[0] == "S":
            steps[step[:2]](i)
        elif step[0] == "T":
            steps[step[:2]](int(step[2]), i)
        elif step[0] == "L":
            load()
        elif step[0] == "N":
            for cp in mom_out:
                cp.start()
        elif step[0] == "M":
            m0()
            for cp in trial_out:
                cp.start()
        elif step[0] == "P":
            pack(i)
        elif step[0] == "X":
            x_step()
        elif step[0] == "Y":
            y_step()
        elif step[0] == "C":
            c_step(i)
        elif step[0] == "E":
            e_step(i)
    finish()
    for cp in sent:
        if id(cp) not in left:
            cp.wait_send()


def body(trial, screened, density, pair_rows, pair_cols, slot_momentum, slot_count):
    smem = pl.BlockSpec(memory_space=pltpu.SMEM)
    anywhere = pl.BlockSpec(memory_space=pl.ANY)
    vmem = pl.BlockSpec(memory_space=pltpu.VMEM)
    dma = pltpu.SemaphoreType.DMA
    return pl.pallas_call(
        kernel,
        out_shape=jax.ShapeDtypeStruct((2, 512), F32),
        in_specs=[anywhere, anywhere, smem, smem, smem, smem, vmem],
        out_specs=vmem,
        scratch_shapes=[
            pltpu.VMEM((16, 128), BF),
            pltpu.VMEM((16, 128), F32),
            pltpu.VMEM((128, 512), BF),
            pltpu.VMEM((8, 128), jnp.int32),
            pltpu.VMEM((3, 8, 8, 128), jnp.int32),
            pltpu.SMEM((3, 8, 8, 128), jnp.int32),
            *[pltpu.VMEM((4, 4, 16, 16, 128), BF)] * NU,
            *[pltpu.VMEM((4, 16, RC, 128), BF)] * (2 * NC),
            pltpu.VMEM((NU, 7, 2, 16, 16, 128), BF),
            pltpu.VMEM((8, NU, 2, 16, 16, 128), BF),
            pltpu.VMEM((8, NC, 2, 16, 16, 128), BF),
            pltpu.VMEM((8, NC, 2, 16, 16, 128), BF),
            pltpu.VMEM((8, 16, 128, 256), BF),
            pltpu.VMEM((8, 16, 128, 256), BF),
            pltpu.VMEM((16, 128, 128), F32),
            pltpu.VMEM((16, 16, 128), BF),
            pltpu.VMEM((8, 16, 128), BF),
            pltpu.VMEM((32, 8, 128), F32),
            pltpu.VMEM((16, 8, 1024), F32),
            pltpu.VMEM((16, 8, 1024), F32),
            pltpu.VMEM((16, 256, 128), BF),
            pltpu.VMEM((16, 128, 128), BF),
            pltpu.VMEM((4, 64, 128), F32),
            pltpu.VMEM((256, 128), F32),
            pltpu.VMEM((128, 128), F32),
            pltpu.VMEM((16, 16, 128), F32),
            pltpu.VMEM((8, 16, 128), F32),
            dma((3, 7)), dma((3, 7)), dma((NU, 8)), dma((NU, 8)), dma((2, NC, 4)), dma((2, NC, 4)),
            dma((NU + 2 * NC, 7)), dma((NU + 2 * NC, 7)), dma((22,)), dma((22,)), dma((22,)), dma((22,)),
            dma((NU + 2 * NC + 1,)), dma((32,)),
        ],
        compiler_params=pltpu.CompilerParams(
            collective_id=0, has_side_effects=True, vmem_limit_bytes=62 * 2**20
        ),
    )(
        screened, density.reshape(density.shape[0], 16, 128, 128),
        slot_momentum, slot_count, pair_rows, pair_cols, trial,
    )


def solution(mesh):
    return jax.shard_map(
        body,
        mesh=mesh,
        in_specs=(
            P(("kr", "kc"), None),
            P(None, None, "kc"),
            P(("kr", "kc"), None, None),
            P(("kr", "kc")),
            P(("kr", "kc")),
            P(("kr", "kc")),
            P(("kr", "kc")),
        ),
        out_specs=P(("kr", "kc"), None),
        check_vma=False,
    )
```
